32 devices in a mesh: sec: 8 (over y, x, core), lane: 4 (over z).
Axes of the slice: x: 2, y: 2, z: 4, core: 2. Of those that a mesh axis runs over, the one named last changes fastest.
Arguments:
- queries: bfloat16 [8, 384, 5120], P('sec', None, 'lane'), may hold values from -40 to 40
- key_value: bfloat16 [2048, 2, 1024], P('sec', None, 'lane'), may hold values from -6 to 6
- grad_out: bfloat16 [8, 384, 5120], P('sec', None, 'lane'), may hold values from -12 to 12
- inputs: bfloat16 [2048, 5120], P('sec'), may hold values from -6 to 6
- w_kv: bfloat16 [5120, 2, 1024], P('sec'), may hold values from -0.078125 to 0.078125
Outputs:
- grad_queries: bfloat16 [8, 384, 5120], P('sec', None, 'lane')
- grad_inputs: bfloat16 [2048, 5120], P(('sec', 'lane'))
- grad_w_kv: float32 [5120, 2, 1024], P('sec', None, 'lane')
The draws below stay inside these ranges and needn't reach their ends.
All inputs are finite; a program needn't handle non-finite values.
Results may differ from the reference program's by a relative error of at most 0.0058.
Values may be sent and summed in bfloat16 or wider, within the bound.
No kernel may reach another device: no remote copies, remote signals or barrier semaphores. Data moves between devices by JAX's collectives and lax.ppermute only.
A program may use at most 128 MiB of HBM per device.

```python
import math
import jax
import jax.numpy as jnp
from jax import lax

D = 5120
NQH = 40
KVH = 8
HD = 128
QLEN = 384
SECS = 8
POS = 2048


def joint_draw(key):
    base = jax.random.fold_in(key, 101)
    keys = jnp.clip(jax.random.normal(jax.random.fold_in(base, 1), (POS, KVH, HD), jnp.float32), -4.0, 4.0)
    queries = jnp.clip(1.5 * jax.random.normal(jax.random.fold_in(base, 2), (SECS, QLEN, NQH, HD), jnp.float32), -6.0, 6.0)
    values = jnp.clip(jax.random.normal(jax.random.fold_in(base, 3), (POS, KVH, HD), jnp.float32), -6.0, 6.0)
    stacked = jnp.stack([keys.reshape(POS, KVH * HD), values.reshape(POS, KVH * HD)], axis=1)
    return (queries.reshape(SECS, QLEN, NQH * HD), stacked)


def draw_queries(key, part):
    return joint_draw(key)[0].astype(jnp.bfloat16)


def draw_key_value(key, part):
    return joint_draw(key)[1].astype(jnp.bfloat16)


def block_scale(key, dims, cuts, least, largest):
    loudness, own = 1.0, jax.random.fold_in(key, 6)
    for axis_at, blocks in cuts:
        steps = jnp.exp(jax.random.uniform(jax.random.fold_in(own, axis_at), (blocks,), jnp.float32, least / len(cuts), largest / len(cuts)))
        loudness = loudness * jnp.repeat(steps, dims[axis_at] // blocks).reshape([-1 if axis == axis_at else 1 for axis in range(len(dims))])
    return loudness


def scatter_about(key, shape, deviation, reach, shards=(), kind=jnp.bfloat16):
    entries = jax.random.normal(key, shape, jnp.float32) * deviation
    if len(shards) > 0:
        entries = block_scale(key, shape, shards, -0.22, 0.18) * entries
    return jnp.clip(entries, min=-reach, max=reach).astype(kind)


def setup_inputs(seed: int = 0) -> dict:
    seeds = jax.random.split(jax.random.key(seed), 6)
    return {
        "queries": draw_queries(jax.random.fold_in(seeds[5], 71), 0),
        "key_value": draw_key_value(jax.random.fold_in(seeds[5], 71), 0),
        "grad_out": scatter_about(seeds[2], (SECS, QLEN, NQH * HD), 2.0, 12.0, ((0, 8), (2, 4))),
        "inputs": scatter_about(seeds[3], (POS, D), 1.0, 6.0, ((0, 8),)),
        "w_kv": scatter_about(seeds[4], (D, 2, KVH * HD), D ** -0.5, 0.078125, ((0, 8),)),
    }


def row_stats(raw, dprobs, block_count):
    rows = raw.shape[0]
    width = raw.shape[1] // block_count
    raw_blocks = raw.reshape(rows, block_count, width).transpose(1, 0, 2)
    dp_blocks = dprobs.reshape(rows, block_count, width).transpose(1, 0, 2)

    def step(carry, items):
        run_max, run_sum, run_dot = carry
        masked, dp_block = items
        new_max = jnp.maximum(run_max, jnp.max(masked, axis=1))
        factor = jnp.exp(run_max - new_max)
        weights = jnp.exp(masked - new_max[:, None])
        run_sum = run_sum * factor + jnp.sum(weights, axis=1)
        run_dot = run_dot * factor + jnp.sum(weights * dp_block, axis=1)
        return (new_max, run_sum, run_dot), None

    start_max = jnp.full((rows,), -1e30, jnp.float32)
    start_zero = jnp.zeros((rows,), jnp.float32)
    (run_max, run_sum, run_dot), _ = lax.scan(step, (start_max, start_zero, start_zero), (raw_blocks, dp_blocks))
    return run_max + jnp.log(run_sum), run_dot / run_sum


def reference(queries, key_value, grad_out, inputs, w_kv):
    group_size = NQH // KVH
    softmax_scale = HD ** -0.5
    keys = key_value[:, 0]
    values = key_value[:, 1]
    block_count = math.gcd(POS, max(1, POS // 512))
    last_key = POS - QLEN + jnp.arange(QLEN * group_size) // group_size
    visible = jnp.arange(POS)[None, :] <= last_key[:, None]

    def section(carry, items):
        query_sec, grad_sec = items
        dq_list = []
        dk_list = []
        dv_list = []
        for kv_head in range(KVH):
            q_rows = query_sec[:, kv_head * group_size * HD:(kv_head + 1) * group_size * HD].reshape(QLEN * group_size, HD)
            do_rows = grad_sec[:, kv_head * group_size * HD:(kv_head + 1) * group_size * HD].reshape(QLEN * group_size, HD)
            k_head = keys[:, kv_head * HD:(kv_head + 1) * HD]
            v_head = values[:, kv_head * HD:(kv_head + 1) * HD]
            raw = jnp.dot(q_rows, k_head.T, preferred_element_type=jnp.float32) * softmax_scale
            raw = jnp.where(visible, raw, -jnp.inf)
            dprobs = jnp.dot(do_rows, v_head.T, preferred_element_type=jnp.float32)
            lse, row_delta = row_stats(raw, dprobs, block_count)
            probs = jnp.where(visible, jnp.exp(raw - lse[:, None]), 0.0)
            dscores = (probs * (dprobs - row_delta[:, None])).astype(jnp.bfloat16)
            probs_low = probs.astype(jnp.bfloat16)
            dq_head = jnp.dot(dscores, k_head, preferred_element_type=jnp.float32) * softmax_scale
            dq_list.append(dq_head.reshape(QLEN, group_size * HD))
            dk_list.append(jnp.dot(dscores.T, q_rows, preferred_element_type=jnp.float32) * softmax_scale)
            dv_list.append(jnp.dot(probs_low.T, do_rows, preferred_element_type=jnp.float32))
        part = jnp.stack([jnp.concatenate(dk_list, axis=1), jnp.concatenate(dv_list, axis=1)], axis=1)
        return carry + part, jnp.concatenate(dq_list, axis=1).astype(jnp.bfloat16)

    start_sum = jnp.zeros((POS, 2, KVH * HD), jnp.float32)
    total, grad_queries = lax.scan(section, start_sum, (queries, grad_out))
    dkv = total.astype(jnp.bfloat16)
    flat_grads = dkv.reshape(POS, 2 * KVH * HD)
    flat_weights = w_kv.reshape(D, 2 * KVH * HD)
    grad_inputs = jnp.dot(flat_grads, flat_weights.T, preferred_element_type=jnp.float32).astype(jnp.bfloat16)
    grad_w_kv = jnp.dot(inputs.T, flat_grads, preferred_element_type=jnp.float32).reshape(D, 2, KVH * HD)
    return grad_queries, grad_inputs, grad_w_kv
```

```python
import functools

import jax
import jax.numpy as jnp
from jax import lax
from jax.experimental import pallas as pl
from jax.experimental.pallas import tpu as pltpu
from jax.sharding import PartitionSpec as P

NQH = 40
KVH = 8
HD = 128
LOG2E = 1.4426950408889634
F32 = jnp.float32
BF16 = jnp.bfloat16
NN = (((1,), (0,)), ((), ()))
NT = (((1,), (1,)), ((), ()))
TN = (((0,), (0,)), ((), ()))
VMEM_BYTES = 48 * 1024 * 1024


def dot(a, b, dims):
    return lax.dot_general(a, b, dims, preferred_element_type=F32)


def params():
    return pltpu.CompilerParams(vmem_limit_bytes=VMEM_BYTES)


def exchange(x, offset, axis):
    return lax.ppermute(x, axis, [(i, i ^ offset) for i in range(lax.axis_size(axis))])


def attend_kernel(n, first, last, place, *refs):
    kv = refs[:n]
    refs = refs[n:]
    q_ref, do_ref = refs[:2]
    refs = refs[2:]
    if not first:
        before_ref = refs[0]
        refs = refs[1:]
    if last:
        dq_ref, keep_ref, send_ref, k_s, v_s, s_s, dp_s, acc = refs[-8:]
    else:
        dq_ref, acc, k_s, v_s, s_s, dp_s = refs[-6:]
    blk = kv[0].shape[0]
    qlen = q_ref.shape[0]
    scale = HD**-0.5
    first_query = n * blk - qlen
    step = pl.program_id(0)
    me = place[0]

    @pl.when(step == 0)
    def _():
        for b in range(n):
            g = lax.bitwise_xor(me, b)
            k_s[g] = kv[b][:, :HD]
            v_s[g] = kv[b][:, HD:]
        if first:
            acc[...] = jnp.zeros_like(acc)
        else:
            acc[...] = before_ref[...]

    q = q_ref[...]
    do = do_ref[...]

    def fold(x, op):
        return op(x.reshape(blk // 8, 8, qlen), axis=0)

    top = None
    for g in range(n):
        s = dot(k_s[g], q, NT)
        if (g + 1) * blk - 1 > first_query:
            key = g * blk + lax.broadcasted_iota(jnp.int32, s.shape, 0)
            row = first_query + lax.broadcasted_iota(jnp.int32, s.shape, 1)
            s = jnp.where(key <= row, s, -jnp.inf)
        s_s[g] = s
        high = fold(s, jnp.max)
        top = high if top is None else jnp.maximum(top, high)
    factor = scale * LOG2E
    top = jnp.max(top, axis=0, keepdims=True) * factor
    total = jnp.zeros((8, qlen), F32)
    weighted = jnp.zeros((8, qlen), F32)
    for g in range(n):
        p = jnp.exp2(s_s[g] * factor - top)
        s_s[g] = p
        dp = dot(v_s[g], do, NT)
        dp_s[g] = dp
        total = total + fold(p, jnp.sum)
        weighted = weighted + fold(p * dp, jnp.sum)
    inverse = 1.0 / jnp.sum(total, axis=0, keepdims=True)
    delta = jnp.sum(weighted, axis=0, keepdims=True) * inverse
    dq = None
    for g in range(n):
        p = s_s[g] * inverse
        ds = (p * (dp_s[g] - delta)).astype(BF16)
        acc[g, :, HD:] += dot(p.astype(BF16), do, NN)
        acc[g, :, :HD] += dot(ds, q, NN)
        part = dot(ds, k_s[g], TN)
        dq = part if dq is None else dq + part
    dq_ref[...] = (dq * scale).astype(BF16)

    if last:

        @pl.when(step == pl.num_programs(0) - 1)
        def _():
            for b in range(n):
                g = lax.bitwise_xor(me, b)
                dk = acc[g, :, :HD] * scale
                dv = acc[g, :, HD:]
                if b % 2:
                    send_ref[b // 2, :, :HD] = dk.astype(BF16)
                    send_ref[b // 2, :, HD:] = dv.astype(BF16)
                else:
                    keep_ref[b // 2, :, :HD] = dk
                    keep_ref[b // 2, :, HD:] = dv


def attend(place, kv, q, do, dq, before, low, count, last):
    n = len(kv)
    blk, width = kv[0].shape
    qlen = q.shape[0]
    whole = lambda shape: pl.BlockSpec(shape, lambda h, s: (0,) * len(shape))
    column = pl.BlockSpec((qlen, HD), lambda h, s: (0, low + h))
    first = before is None
    operands = [*kv, q, do]
    in_specs = [whole((blk, width))] * n + [column, column]
    if not first:
        operands.append(before)
        in_specs.append(whole((n, blk, width)))
    aliases = {}
    if dq is not None:
        aliases = {1 + len(operands): 0}
        operands.append(dq)
        in_specs.append(pl.BlockSpec(memory_space=pl.ANY))
    out_shape = [jax.ShapeDtypeStruct(q.shape, BF16)]
    out_specs = [column]
    scratch = [
        pltpu.VMEM((n, blk, HD), BF16),
        pltpu.VMEM((n, blk, HD), BF16),
        pltpu.VMEM((n, blk, qlen), F32),
        pltpu.VMEM((n, blk, qlen), F32),
    ]
    if last:
        out_shape += [
            jax.ShapeDtypeStruct((n // 2, blk, width), F32),
            jax.ShapeDtypeStruct((n // 2, blk, width), BF16),
        ]
        out_specs += [whole((n // 2, blk, width))] * 2
        scratch.append(pltpu.VMEM((n, blk, width), F32))
    else:
        out_shape.append(jax.ShapeDtypeStruct((n, blk, width), F32))
        out_specs.append(whole((n, blk, width)))
    work = count * qlen * n * blk * HD * 2 * 5
    return pl.pallas_call(
        functools.partial(attend_kernel, n, first, last),
        grid_spec=pltpu.PrefetchScalarGridSpec(
            num_scalar_prefetch=1,
            grid=(count,),
            in_specs=in_specs,
            out_specs=out_specs,
            scratch_shapes=scratch,
        ),
        out_shape=out_shape,
        input_output_aliases=aliases,
        compiler_params=params(),
        cost_estimate=pl.CostEstimate(
            flops=work * 2, bytes_accessed=8 * n * blk * width, transcendentals=0
        ),
        name="attend",
    )(place, *operands)


def pair_sum_kernel(keep_ref, got_ref, own_ref, *send_refs):
    own_ref[...] = keep_ref[0] + got_ref[0].astype(F32)
    for k, send_ref in enumerate(send_refs, 1):
        send_ref[...] = (keep_ref[k] + got_ref[k].astype(F32)).astype(BF16)


def pair_sum(keep, got):
    half, blk, width = keep.shape
    out_shape = [jax.ShapeDtypeStruct((blk, width), F32)]
    out_shape += [jax.ShapeDtypeStruct((blk, width), BF16)] * (half - 1)
    return pl.pallas_call(
        pair_sum_kernel, out_shape=out_shape, compiler_params=params(), name="pair_sum"
    )(keep, got)


def owner_sum_kernel(lanes, place, own_ref, *refs):
    got_refs = refs[: -1 - lanes]
    sum_ref, lane_refs = refs[-1 - lanes], refs[-lanes:]
    total = own_ref[...]
    for got_ref in got_refs:
        total = total + got_ref[...].astype(F32)
    sum_ref[...] = total.astype(BF16)
    rows = lane_refs[0].shape[0]
    for b, lane_ref in enumerate(lane_refs):
        start = pl.multiple_of(lax.bitwise_xor(place[1], b) * rows, rows)
        lane_ref[...] = sum_ref[pl.ds(start, rows), :]


def owner_sum(place, own, got, lanes):
    blk, width = own.shape
    out_shape = [jax.ShapeDtypeStruct((blk, width), BF16)]
    out_shape += [jax.ShapeDtypeStruct((blk // lanes, width), BF16)] * lanes
    return pl.pallas_call(
        functools.partial(owner_sum_kernel, lanes),
        in_specs=[pl.BlockSpec(memory_space=pltpu.SMEM)]
        + [pl.BlockSpec(memory_space=pltpu.VMEM)] * (1 + len(got)),
        out_shape=out_shape,
        compiler_params=params(),
        name="owner_sum",
    )(place, own, *got)


def weight_grad_kernel(heads, half, *refs):
    n = 2 * half
    x_refs, refs = refs[:n], refs[n:]
    out_ref = refs[-1]
    for a in range(heads):
        even, odd = refs[a * (half + 1) : a * (half + 1) + half], refs[a * (half + 1) + half]
        total = None
        for b in range(n):
            grads = odd[b // 2] if b % 2 else even[b // 2][...]
            part = dot(x_refs[b][...], grads, TN)
            total = part if total is None else total + part
        out_ref[:, 0, a * HD : (a + 1) * HD] = total[:, :HD]
        out_ref[:, 1, a * HD : (a + 1) * HD] = total[:, HD:]


def weight_grad(columns, gathered):
    half = len(columns) // 2
    heads = len(gathered)
    operands = list(columns)
    for blocks in gathered:
        operands += blocks
    return pl.pallas_call(
        functools.partial(weight_grad_kernel, heads, half),
        out_shape=jax.ShapeDtypeStruct((columns[0].shape[1], 2, heads * HD), F32),
        compiler_params=params(),
        name="weight_grad",
    )(*operands)


def input_grad_kernel(heads, half, lanes, place, *refs):
    block_refs, refs = refs[: heads * half], refs[heads * half :]
    w_refs, out_refs, left = refs[:2], refs[2 : 2 + half], refs[2 + half]
    me, lane = place[0], place[1]
    rows = block_refs[0].shape[1]
    width = w_refs[0].shape[0]
    features = w_refs[0].shape[1] // 2
    for a in range(heads):
        for k in range(half):
            for b in range(lanes):
                head = lax.bitwise_xor(lane, b) * heads + a
                block = block_refs[a * half + k][b]
                for c in range(2):
                    start = pl.multiple_of(c * features + head * HD, HD)
                    left[k * rows : (k + 1) * rows, pl.ds(start, HD)] = block[:, c * HD : (c + 1) * HD]
    mine = lax.rem(me, 2)
    for order, w_ref in enumerate(w_refs):
        start = pl.multiple_of(lax.bitwise_xor(mine, order) * width, HD)
        result = dot(left[...], w_ref[...], NT).astype(BF16)
        for k in range(half):
            out_refs[k][:, pl.ds(start, width)] = result[k * rows : (k + 1) * rows]


def input_grad(place, blocks, own_w, other_w):
    heads, half = len(blocks), len(blocks[0])
    lanes, rows, _ = blocks[0][0].shape
    width, features = own_w.shape
    flat = [block for head in blocks for block in head]
    return pl.pallas_call(
        functools.partial(input_grad_kernel, heads, half, lanes),
        in_specs=[pl.BlockSpec(memory_space=pltpu.SMEM)]
        + [pl.BlockSpec(memory_space=pltpu.VMEM)] * (len(flat) + 2),
        out_shape=[jax.ShapeDtypeStruct((rows, 2 * width), BF16)] * half,
        scratch_shapes=[pltpu.VMEM((half * rows, features), BF16)],
        compiler_params=params(),
        name="input_grad",
    )(place, *flat, own_w, other_w)


def lay_rows_kernel(place, *refs):
    blocks, out_ref = refs[:-1], refs[-1]
    width = blocks[0].shape[1]
    chip = lax.div(place[0], 2)
    for k, block in enumerate(blocks):
        start = pl.multiple_of(lax.bitwise_xor(chip, k) * width, HD)
        out_ref[:, pl.ds(start, width)] = block[...]


def lay_rows(place, blocks):
    rows, width = blocks[0].shape
    return pl.pallas_call(
        lay_rows_kernel,
        in_specs=[pl.BlockSpec(memory_space=pltpu.SMEM)]
        + [pl.BlockSpec(memory_space=pltpu.VMEM)] * len(blocks),
        out_shape=jax.ShapeDtypeStruct((rows, width * len(blocks)), BF16),
        compiler_params=params(),
        name="lay_rows",
    )(place, *blocks)


def local(queries, key_value, grad_out, inputs, w_kv):
    n = lax.axis_size("sec")
    lanes = lax.axis_size("lane")
    me = lax.axis_index("sec")
    place = jnp.stack([me, lax.axis_index("lane")]).astype(jnp.int32)
    heads = key_value.shape[2] // HD
    group = NQH // KVH
    half = n // 2
    q, do = queries[0], grad_out[0]

    kv = []
    for a in range(heads):
        own = jnp.concatenate([key_value[:, c, a * HD : (a + 1) * HD] for c in range(2)], axis=1)
        blocks = [own] + [exchange(own, 2 * k, "sec") for k in range(1, half)]
        kv.append([x for block in blocks for x in (block, exchange(block, 1, "sec"))])

    cols = inputs.shape[1] // n
    columns = []
    for b in range(n):
        part = lax.dynamic_slice_in_dim(inputs, lax.bitwise_xor(me, b) * cols, cols, axis=1)
        columns.append(exchange(part, b, "sec") if b else part)
    own_w = w_kv.reshape(w_kv.shape[0], -1)
    other_w = exchange(own_w, 1, "sec")

    dq = None
    sums = []
    for a in range(heads):
        pieces = [group]
        before = None
        low = a * group
        for i, count in enumerate(pieces):
            last = i == len(pieces) - 1
            out = attend(place, kv[a], q, do, dq, before, low, count, last)
            dq = out[0]
            low += count
            if not last:
                before = out[1]
        sums.append(out[1:])

    gathered, blocks = [], []
    for keep, send in sums:
        own, *sends = pair_sum(keep, exchange(send, 1, "sec"))
        got = [exchange(x, 2 * k, "sec") for k, x in enumerate(sends, 1)]
        mine, *by_lane = owner_sum(place, own, got, lanes)
        even = [mine] + [exchange(mine, 2 * k, "sec") for k in range(1, half)]
        odd = exchange(jnp.stack(even), 1, "sec")
        gathered.append([*even, odd])
        all_lanes = jnp.stack([by_lane[0]] + [exchange(by_lane[b], b, "lane") for b in range(1, lanes)])
        blocks.append([all_lanes] + [exchange(all_lanes, 2 * k, "sec") for k in range(1, half)])

    rows = input_grad(place, blocks, own_w, other_w)
    rows = [rows[0]] + [exchange(rows[k], 2 * k, "sec") for k in range(1, half)]
    grad_inputs = lay_rows(place, rows)
    grad_w_kv = weight_grad(columns, gathered)
    return dq[None], grad_inputs, grad_w_kv


def solution(mesh):
    in_specs = (
        P("sec", None, "lane"),
        P("sec", None, "lane"),
        P("sec", None, "lane"),
        P("sec", None),
        P("sec", None, None),
    )
    out_specs = (P("sec", None, "lane"), P(("sec", "lane"), None), P("sec", None, "lane"))
    return jax.shard_map(local, mesh=mesh, in_specs=in_specs, out_specs=out_specs, check_vma=False)
```

```python
import functools

import jax
import jax.numpy as jnp
from jax import lax
from jax.experimental import pallas as pl
from jax.experimental.pallas import tpu as pltpu
from jax.sharding import PartitionSpec as P

NQH = 40
KVH = 8
HD = 128
LOG2E = 1.4426950408889634
F32 = jnp.float32
BF16 = jnp.bfloat16
NN = (((1,), (0,)), ((), ()))
NT = (((1,), (1,)), ((), ()))
TN = (((0,), (0,)), ((), ()))
VMEM_BYTES = 24 * 1024 * 1024
ATTEND_VMEM_BYTES = 52 * 1024 * 1024


def dot(a, b, dims):
    return lax.dot_general(a, b, dims, preferred_element_type=F32)


def params(limit=VMEM_BYTES):
    return pltpu.CompilerParams(vmem_limit_bytes=limit)


def exchange(x, offset, axis):
    return lax.ppermute(x, axis, [(i, i ^ offset) for i in range(lax.axis_size(axis))])


def attend_kernel(n, first, last, place, *refs):
    kv = refs[:n]
    refs = refs[n:]
    q_ref, do_ref = refs[:2]
    refs = refs[2:]
    if not first:
        before_ref = refs[0]
        refs = refs[1:]
    if last:
        dq_ref, keep_ref, send_ref, k_s, v_s, s_s, dp_s, acc = refs[-8:]
    else:
        dq_ref, acc, k_s, v_s, s_s, dp_s = refs[-6:]
    blk = kv[0].shape[0]
    qlen = q_ref.shape[0]
    scale = HD**-0.5
    first_query = n * blk - qlen
    step = pl.program_id(0)
    me = place[0]

    @pl.when(step == 0)
    def _():
        for b in range(n):
            g = lax.bitwise_xor(me, b)
            k_s[g] = kv[b][:, :HD]
            v_s[g] = kv[b][:, HD:]
        if first:
            acc[...] = jnp.zeros_like(acc)
        else:
            acc[...] = before_ref[...]

    q = q_ref[...]
    do = do_ref[...]

    def fold(x, op):
        return op(x.reshape(blk // 8, 8, qlen), axis=0)

    top = None
    for g in range(n):
        s = dot(k_s[g], q, NT)
        if (g + 1) * blk - 1 > first_query:
            key = g * blk + lax.broadcasted_iota(jnp.int32, s.shape, 0)
            row = first_query + lax.broadcasted_iota(jnp.int32, s.shape, 1)
            s = jnp.where(key <= row, s, -jnp.inf)
        s_s[g] = s
        high = fold(s, jnp.max)
        top = high if top is None else jnp.maximum(top, high)
    factor = scale * LOG2E
    top = jnp.max(top, axis=0, keepdims=True) * factor
    total = jnp.zeros((8, qlen), F32)
    weighted = jnp.zeros((8, qlen), F32)
    for g in range(n):
        p = jnp.exp2(s_s[g] * factor - top)
        s_s[g] = p
        dp = dot(v_s[g], do, NT)
        dp_s[g] = dp
        total = total + fold(p, jnp.sum)
        weighted = weighted + fold(p * dp, jnp.sum)
    inverse = 1.0 / jnp.sum(total, axis=0, keepdims=True)
    delta = jnp.sum(weighted, axis=0, keepdims=True) * inverse
    dq = None
    for g in range(n):
        p = s_s[g] * inverse
        ds = (p * (dp_s[g] - delta)).astype(BF16)
        acc[g, :, HD:] += dot(p.astype(BF16), do, NN)
        acc[g, :, :HD] += dot(ds, q, NN)
        part = dot(ds, k_s[g], TN)
        dq = part if dq is None else dq + part
    dq_ref[...] = (dq * scale).astype(BF16)

    if last:

        @pl.when(step == pl.num_programs(0) - 1)
        def _():
            for b in range(n):
                g = lax.bitwise_xor(me, b)
                dk = acc[g, :, :HD] * scale
                dv = acc[g, :, HD:]
                if b % 2:
                    send_ref[b // 2, :, :HD] = dk.astype(BF16)
                    send_ref[b // 2, :, HD:] = dv.astype(BF16)
                else:
                    keep_ref[b // 2, :, :HD] = dk
                    keep_ref[b // 2, :, HD:] = dv


def attend(place, kv, head, q, do, dq, before, low, count, last):
    n = len(kv)
    blk, width = kv[0].shape[0], 2 * HD
    qlen = q.shape[0]
    whole = lambda shape: pl.BlockSpec(shape, lambda h, s: (0,) * len(shape))
    column = pl.BlockSpec((qlen, HD), lambda h, s: (0, low + h))
    first = before is None
    operands = [*kv, q, do]
    in_specs = [pl.BlockSpec((blk, width), lambda h, s: (0, head))] * n + [column, column]
    if not first:
        operands.append(before)
        in_specs.append(whole((n, blk, width)))
    aliases = {}
    if dq is not None:
        aliases = {1 + len(operands): 0}
        operands.append(dq)
        in_specs.append(pl.BlockSpec(memory_space=pl.ANY))
    out_shape = [jax.ShapeDtypeStruct(q.shape, BF16)]
    out_specs = [column]
    scratch = [
        pltpu.VMEM((n, blk, HD), BF16),
        pltpu.VMEM((n, blk, HD), BF16),
        pltpu.VMEM((n, blk, qlen), F32),
        pltpu.VMEM((n, blk, qlen), F32),
    ]
    if last:
        out_shape += [
            jax.ShapeDtypeStruct((n // 2, blk, width), F32),
            jax.ShapeDtypeStruct((n // 2, blk, width), BF16),
        ]
        out_specs += [whole((n // 2, blk, width))] * 2
        scratch.append(pltpu.VMEM((n, blk, width), F32))
    else:
        out_shape.append(jax.ShapeDtypeStruct((n, blk, width), F32))
        out_specs.append(whole((n, blk, width)))
    work = count * qlen * n * blk * HD * 2 * 5
    return pl.pallas_call(
        functools.partial(attend_kernel, n, first, last),
        grid_spec=pltpu.PrefetchScalarGridSpec(
            num_scalar_prefetch=1,
            grid=(count,),
            in_specs=in_specs,
            out_specs=out_specs,
            scratch_shapes=scratch,
        ),
        out_shape=out_shape,
        input_output_aliases=aliases,
        compiler_params=params(ATTEND_VMEM_BYTES),
        cost_estimate=pl.CostEstimate(
            flops=work * 2, bytes_accessed=8 * n * blk * width, transcendentals=0
        ),
        name="attend",
    )(place, *operands)


def pair_sum_kernel(heads, *refs):
    keeps, gots, own_ref, send_refs = refs[:heads], refs[heads : 2 * heads], refs[2 * heads], refs[2 * heads + 1 :]
    for a in range(heads):
        span = pl.ds(a * 2 * HD, 2 * HD)
        own_ref[:, span] = keeps[a][0] + gots[a][0].astype(F32)
        for k, send_ref in enumerate(send_refs, 1):
            send_ref[:, span] = (keeps[a][k] + gots[a][k].astype(F32)).astype(BF16)


def pair_sum(keeps, gots):
    half, blk, width = keeps[0].shape
    heads = len(keeps)
    out_shape = [jax.ShapeDtypeStruct((blk, heads * width), F32)]
    out_shape += [jax.ShapeDtypeStruct((blk, heads * width), BF16)] * (half - 1)
    return pl.pallas_call(
        functools.partial(pair_sum_kernel, heads),
        out_shape=out_shape,
        compiler_params=params(),
        name="pair_sum",
    )(*keeps, *gots)


def owner_sum_kernel(lanes, place, own_ref, *refs):
    got_refs = refs[: -1 - lanes]
    sum_ref, lane_refs = refs[-1 - lanes], refs[-lanes:]
    total = own_ref[...]
    for got_ref in got_refs:
        total = total + got_ref[...].astype(F32)
    sum_ref[...] = total.astype(BF16)
    rows = lane_refs[0].shape[0]
    for b, lane_ref in enumerate(lane_refs):
        start = pl.multiple_of(lax.bitwise_xor(place[1], b) * rows, rows)
        lane_ref[...] = sum_ref[pl.ds(start, rows), :]


def owner_sum(place, own, got, lanes):
    blk, width = own.shape
    out_shape = [jax.ShapeDtypeStruct((blk, width), BF16)]
    out_shape += [jax.ShapeDtypeStruct((blk // lanes, width), BF16)] * lanes
    return pl.pallas_call(
        functools.partial(owner_sum_kernel, lanes),
        in_specs=[pl.BlockSpec(memory_space=pltpu.SMEM)]
        + [pl.BlockSpec(memory_space=pltpu.VMEM)] * (1 + len(got)),
        out_shape=out_shape,
        compiler_params=params(),
        name="owner_sum",
    )(place, own, *got)


def weight_grad_kernel(half, place, *refs):
    x_refs, grad_refs, keep_ref, send_ref = refs[:half], refs[half : 2 * half], refs[2 * half], refs[2 * half + 1]
    cols = keep_ref.shape[0]
    mine = lax.rem(place[0], 2)
    for order, out_ref in enumerate((keep_ref, send_ref)):
        start = pl.multiple_of(lax.bitwise_xor(mine, order) * cols, HD)
        total = None
        for x_ref, grad_ref in zip(x_refs, grad_refs):
            part = dot(x_ref[:, pl.ds(start, cols)], grad_ref[...], TN)
            total = part if total is None else total + part
        out_ref[...] = total


def weight_grad(place, columns, gathered):
    half = len(columns)
    cols = columns[0].shape[1] // 2
    shape = jax.ShapeDtypeStruct((cols, gathered[0].shape[1]), F32)
    return pl.pallas_call(
        functools.partial(weight_grad_kernel, half),
        in_specs=[pl.BlockSpec(memory_space=pltpu.SMEM)] + [pl.BlockSpec(memory_space=pltpu.VMEM)] * (2 * half),
        out_shape=[shape, shape],
        compiler_params=params(),
        name="weight_grad",
    )(place, *columns, *gathered)


def weight_sum_kernel(heads, keep_ref, got_ref, out_ref):
    for a in range(heads):
        for c in range(2):
            span = pl.ds((2 * a + c) * HD, HD)
            out_ref[:, c, a * HD : (a + 1) * HD] = keep_ref[:, span] + got_ref[:, span]


def weight_sum(keep, got):
    cols, features = keep.shape
    heads = features // (2 * HD)
    return pl.pallas_call(
        functools.partial(weight_sum_kernel, heads),
        out_shape=jax.ShapeDtypeStruct((cols, 2, heads * HD), F32),
        compiler_params=params(),
        name="weight_sum",
    )(keep, got)


def input_grad_kernel(heads, half, lanes, place, *refs):
    block_refs, refs = refs[:half], refs[half:]
    w_refs, out_refs, left = refs[:2], refs[2 : 2 + half], refs[2 + half]
    me, lane = place[0], place[1]
    rows = block_refs[0].shape[1]
    width = w_refs[0].shape[0]
    features = w_refs[0].shape[1] // 2
    for k in range(half):
        for b in range(lanes):
            for a in range(heads):
                head = lax.bitwise_xor(lane, b) * heads + a
                for c in range(2):
                    start = pl.multiple_of(c * features + head * HD, HD)
                    span = pl.ds((2 * a + c) * HD, HD)
                    left[k * rows : (k + 1) * rows, pl.ds(start, HD)] = block_refs[k][b, :, span]
    mine = lax.rem(me, 2)
    for order, w_ref in enumerate(w_refs):
        start = pl.multiple_of(lax.bitwise_xor(mine, order) * width, HD)
        result = dot(left[...], w_ref[...], NT).astype(BF16)
        for k in range(half):
            out_refs[k][:, pl.ds(start, width)] = result[k * rows : (k + 1) * rows]


def input_grad(place, blocks, own_w, other_w):
    half = len(blocks)
    lanes, rows, here = blocks[0].shape
    width, features = own_w.shape
    return pl.pallas_call(
        functools.partial(input_grad_kernel, here // (2 * HD), half, lanes),
        in_specs=[pl.BlockSpec(memory_space=pltpu.SMEM)]
        + [pl.BlockSpec(memory_space=pltpu.VMEM)] * (half + 2),
        out_shape=[jax.ShapeDtypeStruct((rows, 2 * width), BF16)] * half,
        scratch_shapes=[pltpu.VMEM((half * rows, features), BF16)],
        compiler_params=params(),
        name="input_grad",
    )(place, *blocks, own_w, other_w)


def lay_rows_kernel(place, *refs):
    blocks, out_ref = refs[:-1], refs[-1]
    width = blocks[0].shape[1]
    chip = lax.div(place[0], 2)
    for k, block in enumerate(blocks):
        start = pl.multiple_of(lax.bitwise_xor(chip, k) * width, HD)
        out_ref[:, pl.ds(start, width)] = block[...]


def lay_rows(place, blocks):
    rows, width = blocks[0].shape
    return pl.pallas_call(
        lay_rows_kernel,
        in_specs=[pl.BlockSpec(memory_space=pltpu.SMEM)]
        + [pl.BlockSpec(memory_space=pltpu.VMEM)] * len(blocks),
        out_shape=jax.ShapeDtypeStruct((rows, width * len(blocks)), BF16),
        compiler_params=params(),
        name="lay_rows",
    )(place, *blocks)


def local(queries, key_value, grad_out, inputs, w_kv):
    n = lax.axis_size("sec")
    lanes = lax.axis_size("lane")
    me = lax.axis_index("sec")
    place = jnp.stack([me, lax.axis_index("lane")]).astype(jnp.int32)
    heads = key_value.shape[2] // HD
    group = NQH // KVH
    half = n // 2
    q, do = queries[0], grad_out[0]

    def across(blocks):
        return [blocks[0]] + [exchange(blocks[k], 2 * k, "sec") for k in range(1, half)]

    own = jnp.concatenate(
        [key_value[:, c, a * HD : (a + 1) * HD] for a in range(heads) for c in range(2)], axis=1
    )
    near = across([own] * half)
    kv = [x for block in near for x in (block, exchange(block, 1, "sec"))]

    cols = 2 * inputs.shape[1] // n
    inputs, near = lax.optimization_barrier((inputs, near))
    columns = across(
        [
            lax.dynamic_slice_in_dim(inputs, lax.bitwise_xor(me // 2, k) * cols, cols, axis=1)
            for k in range(half)
        ]
    )
    own_w = w_kv.reshape(w_kv.shape[0], -1)
    other_w = exchange(own_w, 1, "sec")

    dq = None
    keeps, gots = [], []
    for a in range(heads):
        dq, keep, send = attend(place, kv, a, q, do, dq, None, a * group, group, True)
        if a == heads - 1:
            send, columns[1:] = lax.optimization_barrier((send, columns[1:]))
        keeps.append(keep)
        gots.append(exchange(send, 1, "sec"))

    own, *sends = pair_sum(keeps, gots)
    own, *got = across([own, *sends])
    mine, *by_lane = owner_sum(place, own, got, lanes)
    by_lane[1:] = [exchange(by_lane[b], b, "lane") for b in range(1, lanes)]
    mine, by_lane[1:-1] = lax.optimization_barrier((mine, by_lane[1:-1]))
    gathered = across([mine] * half)
    blocks = across([jnp.stack(by_lane)] * half)

    rows = input_grad(place, blocks, own_w, other_w)
    rows, gathered = lax.optimization_barrier((rows, gathered))
    rows = across(rows)
    keep, send = weight_grad(place, columns, gathered)
    grad_w_kv = weight_sum(keep, exchange(send, 1, "sec"))
    rows, grad_w_kv = lax.optimization_barrier((rows, grad_w_kv))
    grad_inputs = lay_rows(place, rows)
    return dq[None], grad_inputs, grad_w_kv


def solution(mesh):
    in_specs = (
        P("sec", None, "lane"),
        P("sec", None, "lane"),
        P("sec", None, "lane"),
        P("sec", None),
        P("sec", None, None),
    )
    out_specs = (P("sec", None, "lane"), P(("sec", "lane"), None), P("sec", None, "lane"))
    return jax.shard_map(local, mesh=mesh, in_specs=in_specs, out_specs=out_specs, check_vma=False)
```

```python
import functools

import jax
import jax.numpy as jnp
from jax import lax
from jax.experimental import pallas as pl
from jax.experimental.pallas import tpu as pltpu
from jax.sharding import PartitionSpec as P

NQH = 40
KVH = 8
HD = 128
LOG2E = 1.4426950408889634
F32 = jnp.float32
BF16 = jnp.bfloat16
NN = (((1,), (0,)), ((), ()))
NT = (((1,), (1,)), ((), ()))
TN = (((0,), (0,)), ((), ()))
VMEM_BYTES = 24 * 1024 * 1024
ATTEND_VMEM_BYTES = 16 * 1024
SEG = 128
UNIT = 2


def dot(a, b, dims):
    return lax.dot_general(a, b, dims, preferred_element_type=F32)


def params(limit=VMEM_BYTES):
    return pltpu.CompilerParams(vmem_limit_bytes=limit)


def exchange(x, offset, axis):
    return lax.ppermute(x, axis, [(i, i ^ offset) for i in range(lax.axis_size(axis))])


def key_blocks(keys, qlen):
    first = keys - qlen
    blocks = []
    at = 0
    while at < keys:
        size = 2 * SEG if at + 2 * SEG <= first + SEG else SEG
        blocks.append((at, size, sum(first + qlen - t * SEG > at for t in range(qlen // SEG))))
        at += size
    return blocks


def attend_kernel(n, group, aliased, place, *refs):
    kv, refs = refs[:n], refs[n:]
    q_ref, do_ref = refs[:2]
    dq_ref, keep_ref, send_ref = refs[2 + aliased : 5 + aliased]
    k_s, v_s, q_s, do_s, qt_s, dot_s, s_s, dp_s, top_s, sum_s, weighted_s, acc = refs[5 + aliased :]
    qlen = q_ref.shape[0]
    keys = k_s.shape[0]
    blk = keys // n
    first = keys - qlen
    segments = qlen // SEG
    scale = HD**-0.5
    factor = scale * LOG2E
    me = place[0]

    def place_of(b):
        return pl.multiple_of(lax.bitwise_xor(me, b) * blk, blk)

    for b in range(n):
        k_s[pl.ds(place_of(b), blk), :] = kv[b][:, :HD]
        v_s[pl.ds(place_of(b), blk), :] = kv[b][:, HD:]

    units = [range(h, min(h + UNIT, group)) for h in range(0, group, UNIT)]
    at = 0
    for unit in units:
        for t in range(segments):
            low = qlen - (t + 1) * SEG
            for h in unit:
                x = q_ref[low : low + SEG, h * HD : (h + 1) * HD]
                y = do_ref[low : low + SEG, h * HD : (h + 1) * HD]
                q_s[at : at + SEG, :] = x
                do_s[at : at + SEG, :] = y
                qt_s[:, at : at + SEG] = x.T
                dot_s[:, at : at + SEG] = y.T
                at += SEG

    def spread(x):
        return jnp.broadcast_to(x, (x.shape[0], SEG))

    base = 0
    for index, unit in enumerate(units):
        width = len(unit) * SEG
        whole = width * segments
        blocks = [(k0, size, seen * width) for k0, size, seen in key_blocks(keys, qlen)]

        for k0, size, high in blocks:
            s = dot(q_s[base : base + high, :], k_s[k0 : k0 + size, :], NT)
            top = None
            for k in range(k0, k0 + size, SEG):
                piece = s[:, k - k0 : k - k0 + SEG]
                last = first + qlen - high // width * SEG
                if k + SEG - 1 > last:
                    edge = piece[high - width :]
                    key = k + lax.broadcasted_iota(jnp.int32, edge.shape, 1)
                    row = last + lax.rem(lax.broadcasted_iota(jnp.int32, edge.shape, 0), SEG)
                    edge = jnp.where(key <= row, edge, -jnp.inf)
                    piece = edge if high == width else jnp.concatenate([piece[: high - width], edge], axis=0)
                s_s[:high, k : k + SEG] = piece
                top = piece if top is None else jnp.maximum(top, piece)
            top_s[:high, :] = top if k0 == 0 else jnp.maximum(top_s[:high, :], top)
        top_s[:whole, :] = spread(jnp.max(top_s[:whole, :], axis=1, keepdims=True) * factor)

        for k0, size, high in blocks:
            dp = dot(do_s[base : base + high, :], v_s[k0 : k0 + size, :], NT)
            total = weighted = None
            for k in range(k0, k0 + size, SEG):
                p = jnp.exp2(s_s[:high, k : k + SEG] * factor - top_s[:high, :])
                s_s[:high, k : k + SEG] = p
                piece = dp[:, k - k0 : k - k0 + SEG]
                dp_s[:high, k : k + SEG] = piece
                total = p if total is None else total + p
                weighted = p * piece if weighted is None else weighted + p * piece
            sum_s[:high, :] = total if k0 == 0 else sum_s[:high, :] + total
            weighted_s[:high, :] = weighted if k0 == 0 else weighted_s[:high, :] + weighted
        inverse = 1.0 / jnp.sum(sum_s[:whole, :], axis=1, keepdims=True)
        delta = jnp.sum(weighted_s[:whole, :], axis=1, keepdims=True) * inverse
        sum_s[:whole, :] = spread(inverse)
        weighted_s[:whole, :] = spread(delta)

        dq = None
        for k0, size, high in blocks:
            low_parts, ds_parts = [], []
            for k in range(k0, k0 + size, SEG):
                p = s_s[:high, k : k + SEG] * sum_s[:high, :]
                ds_parts.append((p * (dp_s[:high, k : k + SEG] - weighted_s[:high, :])).astype(BF16))
                low_parts.append(p.astype(BF16))
            low = jnp.concatenate(low_parts, axis=1)
            ds = jnp.concatenate(ds_parts, axis=1)
            dv = dot(dot_s[:, base : base + high], low, NN)
            dk = dot(qt_s[:, base : base + high], ds, NN)
            if index:
                dv = acc[HD:, k0 : k0 + size] + dv
                dk = acc[:HD, k0 : k0 + size] + dk
            acc[HD:, k0 : k0 + size] = dv
            acc[:HD, k0 : k0 + size] = dk
            part = dot(ds, k_s[k0 : k0 + size, :], NN)
            if dq is None:
                dq = part
            elif high == whole:
                dq = dq + part
            else:
                dq = jnp.concatenate([dq[:high] + part, dq[high:]], axis=0)
        dq = (dq * scale).astype(BF16)
        at = 0
        for t in range(segments):
            low = qlen - (t + 1) * SEG
            for h in unit:
                dq_ref[low : low + SEG, h * HD : (h + 1) * HD] = dq[at : at + SEG]
                at += SEG
        base += whole

    for b in range(n):
        dk = acc[:HD, pl.ds(place_of(b), blk)] * scale
        dv = acc[HD:, pl.ds(place_of(b), blk)]
        if b % 2:
            send_ref[b // 2, :HD, :] = dk.astype(BF16)
            send_ref[b // 2, HD:, :] = dv.astype(BF16)
        else:
            keep_ref[b // 2, :HD, :] = dk
            keep_ref[b // 2, HD:, :] = dv


def attend(place, kv, head, q, do, dq, group):
    n = len(kv)
    blk, width = kv[0].shape[0], 2 * HD
    qlen = q.shape[0]
    keys = n * blk
    column = pl.BlockSpec((qlen, group * HD), lambda i, s: (0, head))
    full = lambda shape: pl.BlockSpec(shape, lambda i, s: (0,) * len(shape))
    in_specs = [pl.BlockSpec((blk, width), lambda i, s: (0, head))] * n + [column, column]
    operands = [*kv, q, do]
    aliases = {}
    if dq is not None:
        aliases = {1 + len(operands): 0}
        operands.append(dq)
        in_specs.append(pl.BlockSpec(memory_space=pl.ANY))
    rows = min(UNIT, group) * qlen
    parts = (n // 2, width, blk)
    work = group * qlen * keys * HD * 10
    return pl.pallas_call(
        functools.partial(attend_kernel, n, group, dq is not None),
        grid_spec=pltpu.PrefetchScalarGridSpec(
            num_scalar_prefetch=1,
            grid=(1,),
            in_specs=in_specs,
            out_specs=[column, full(parts), full(parts)],
            scratch_shapes=[
                pltpu.VMEM((keys, HD), BF16),
                pltpu.VMEM((keys, HD), BF16),
                pltpu.VMEM((group * qlen, HD), BF16),
                pltpu.VMEM((group * qlen, HD), BF16),
                pltpu.VMEM((HD, group * qlen), BF16),
                pltpu.VMEM((HD, group * qlen), BF16),
                pltpu.VMEM((rows, keys), F32),
                pltpu.VMEM((rows, keys), F32),
                pltpu.VMEM((rows, SEG), F32),
                pltpu.VMEM((rows, SEG), F32),
                pltpu.VMEM((rows, SEG), F32),
                pltpu.VMEM((width, keys), F32),
            ],
        ),
        out_shape=[
            jax.ShapeDtypeStruct(q.shape, BF16),
            jax.ShapeDtypeStruct(parts, F32),
            jax.ShapeDtypeStruct(parts, BF16),
        ],
        input_output_aliases=aliases,
        compiler_params=params(keys * ATTEND_VMEM_BYTES),
        cost_estimate=pl.CostEstimate(flops=work * 2, bytes_accessed=8 * keys * width, transcendentals=0),
        name="attend",
    )(place, *operands)


def pair_sum_kernel(heads, *refs):
    keeps, gots, own_ref, send_refs = refs[:heads], refs[heads : 2 * heads], refs[2 * heads], refs[2 * heads + 1 :]
    for a in range(heads):
        span = pl.ds(a * 2 * HD, 2 * HD)
        own_ref[span, :] = keeps[a][0] + gots[a][0].astype(F32)
        for k, send_ref in enumerate(send_refs, 1):
            send_ref[span, :] = (keeps[a][k] + gots[a][k].astype(F32)).astype(BF16)


def pair_sum(keeps, gots):
    half, width, blk = keeps[0].shape
    heads = len(keeps)
    out_shape = [jax.ShapeDtypeStruct((heads * width, blk), F32)]
    out_shape += [jax.ShapeDtypeStruct((heads * width, blk), BF16)] * (half - 1)
    return pl.pallas_call(
        functools.partial(pair_sum_kernel, heads),
        out_shape=out_shape,
        compiler_params=params(),
        name="pair_sum",
    )(*keeps, *gots)


def owner_sum_kernel(lanes, place, own_ref, *refs):
    got_refs = refs[: -1 - lanes]
    sum_ref, lane_refs = refs[-1 - lanes], refs[-lanes:]
    total = own_ref[...]
    for got_ref in got_refs:
        total = total + got_ref[...].astype(F32)
    sum_ref[...] = total.astype(BF16).T
    rows = lane_refs[0].shape[0]
    for b, lane_ref in enumerate(lane_refs):
        start = pl.multiple_of(lax.bitwise_xor(place[1], b) * rows, rows)
        lane_ref[...] = sum_ref[pl.ds(start, rows), :]


def owner_sum(place, own, got, lanes):
    width, blk = own.shape
    out_shape = [jax.ShapeDtypeStruct((blk, width), BF16)]
    out_shape += [jax.ShapeDtypeStruct((blk // lanes, width), BF16)] * lanes
    return pl.pallas_call(
        functools.partial(owner_sum_kernel, lanes),
        in_specs=[pl.BlockSpec(memory_space=pltpu.SMEM)]
        + [pl.BlockSpec(memory_space=pltpu.VMEM)] * (1 + len(got)),
        out_shape=out_shape,
        compiler_params=params(),
        name="owner_sum",
    )(place, own, *got)


def weight_grad_kernel(half, place, *refs):
    x_refs, grad_refs, keep_ref, send_ref = refs[:half], refs[half:-2], refs[-2], refs[-1]
    cols = keep_ref.shape[0]
    mine = lax.rem(place[0], 2)
    for order, out_ref in enumerate((keep_ref, send_ref)):
        start = pl.multiple_of(lax.bitwise_xor(mine, order) * cols, HD)
        total = None
        for x_ref, grad_ref in zip(x_refs, grad_refs):
            part = dot(x_ref[:, pl.ds(start, cols)], grad_ref[...], TN)
            total = part if total is None else total + part
        out_ref[...] = total


def weight_grad(place, columns, gathered):
    half = len(columns)
    cols = columns[0].shape[1] // 2
    shape = jax.ShapeDtypeStruct((cols, gathered[0].shape[1]), F32)
    return pl.pallas_call(
        functools.partial(weight_grad_kernel, half),
        in_specs=[pl.BlockSpec(memory_space=pltpu.SMEM)] + [pl.BlockSpec(memory_space=pltpu.VMEM)] * (2 * half),
        out_shape=[shape, shape],
        compiler_params=params(),
        name="weight_grad",
    )(place, *columns, *gathered)


def weight_sum_kernel(heads, keep_ref, got_ref, out_ref):
    for a in range(heads):
        for c in range(2):
            span = pl.ds((2 * a + c) * HD, HD)
            out_ref[:, c, a * HD : (a + 1) * HD] = keep_ref[:, span] + got_ref[:, span]


def weight_sum(keep, got):
    cols, features = keep.shape
    heads = features // (2 * HD)
    return pl.pallas_call(
        functools.partial(weight_sum_kernel, heads),
        out_shape=jax.ShapeDtypeStruct((cols, 2, heads * HD), F32),
        compiler_params=params(),
        name="weight_sum",
    )(keep, got)


def input_grad_kernel(heads, half, lanes, place, *refs):
    block_refs, refs = refs[:half], refs[half:]
    w_refs, out_refs, left = refs[:2], refs[2 : 2 + half], refs[2 + half]
    me, lane = place[0], place[1]
    rows = block_refs[0].shape[1]
    width = w_refs[0].shape[0]
    features = w_refs[0].shape[1] // 2
    for k in range(half):
        for b in range(lanes):
            for a in range(heads):
                head = lax.bitwise_xor(lane, b) * heads + a
                for c in range(2):
                    start = pl.multiple_of(c * features + head * HD, HD)
                    span = pl.ds((2 * a + c) * HD, HD)
                    left[k * rows : (k + 1) * rows, pl.ds(start, HD)] = block_refs[k][b, :, span]
    mine = lax.rem(me, 2)
    for order, w_ref in enumerate(w_refs):
        start = pl.multiple_of(lax.bitwise_xor(mine, order) * width, HD)
        result = dot(left[...], w_ref[...], NT).astype(BF16)
        for k in range(half):
            out_refs[k][:, pl.ds(start, width)] = result[k * rows : (k + 1) * rows]


def input_grad(place, blocks, own_w, other_w):
    half = len(blocks)
    lanes, rows, here = blocks[0].shape
    width, features = own_w.shape
    return pl.pallas_call(
        functools.partial(input_grad_kernel, here // (2 * HD), half, lanes),
        in_specs=[pl.BlockSpec(memory_space=pltpu.SMEM)]
        + [pl.BlockSpec(memory_space=pltpu.VMEM)] * (len(blocks) + 2),
        out_shape=[jax.ShapeDtypeStruct((rows, 2 * width), BF16)] * half,
        scratch_shapes=[pltpu.VMEM((half * rows, features), BF16)],
        compiler_params=params(),
        name="input_grad",
    )(place, *blocks, own_w, other_w)


def lay_rows_kernel(place, *refs):
    blocks, out_ref, sems = refs[:-2], refs[-2], refs[-1]
    width = blocks[0].shape[1]
    chip = lax.div(place[0], 2)
    copies = []
    for k, block in enumerate(blocks):
        start = pl.multiple_of(lax.bitwise_xor(chip, k) * width, HD)
        copies.append(pltpu.make_async_copy(block, out_ref.at[:, pl.ds(start, width)], sems.at[k]))
        copies[-1].start()
    for copy in copies:
        copy.wait()


def lay_rows(place, blocks):
    rows, width = blocks[0].shape
    count = len(blocks)
    return pl.pallas_call(
        lay_rows_kernel,
        in_specs=[pl.BlockSpec(memory_space=pltpu.SMEM)] + [pl.BlockSpec(memory_space=pl.ANY)] * count,
        out_specs=pl.BlockSpec(memory_space=pl.ANY),
        out_shape=jax.ShapeDtypeStruct((rows, width * count), BF16),
        scratch_shapes=[pltpu.SemaphoreType.DMA((count,))],
        compiler_params=params(),
        name="lay_rows",
    )(place, *blocks)


def local(queries, key_value, grad_out, inputs, w_kv):
    n = lax.axis_size("sec")
    lanes = lax.axis_size("lane")
    me = lax.axis_index("sec")
    place = jnp.stack([me, lax.axis_index("lane")]).astype(jnp.int32)
    heads = key_value.shape[2] // HD
    group = NQH // KVH
    half = n // 2
    q, do = queries[0], grad_out[0]

    def across(blocks):
        return [blocks[0]] + [exchange(blocks[k], 2 * k, "sec") for k in range(1, half)]

    own = jnp.concatenate(
        [key_value[:, c, a * HD : (a + 1) * HD] for a in range(heads) for c in range(2)], axis=1
    )
    near = across([own] * half)
    kv = [x for block in near for x in (block, exchange(block, 1, "sec"))]

    cols = 2 * inputs.shape[1] // n
    columns = [
        lax.dynamic_slice_in_dim(inputs, lax.bitwise_xor(me // 2, k) * cols, cols, axis=1)
        for k in range(half)
    ]
    columns, near = lax.optimization_barrier((columns, near))
    columns = across(columns)
    own_w = w_kv.reshape(w_kv.shape[0], -1)
    other_w = exchange(own_w, 1, "sec")

    dq = None
    keeps, gots = [], []
    for a in range(heads):
        dq, keep, send = attend(place, kv, a, q, do, dq, group)
        if a == heads - 1:
            keep, columns[1:] = lax.optimization_barrier((keep, columns[1:]))
        keeps.append(keep)
        gots.append(exchange(send, 1, "sec"))

    own, *sends = pair_sum(keeps, gots)
    _, *got = across([own, *sends])
    mine, *by_lane = owner_sum(place, own, got, lanes)
    by_lane[1:] = [exchange(by_lane[b], b, "lane") for b in range(1, lanes)]
    gathered = across([mine] * half)
    blocks = across([jnp.stack(by_lane)] * half)
    blocks, gathered = lax.optimization_barrier((blocks, gathered))

    rows = list(input_grad(place, blocks, own_w, other_w))
    rows[0], gathered = lax.optimization_barrier((rows[0], gathered))
    rows = across(rows)
    keep, send = weight_grad(place, columns, gathered)
    grad_w_kv = weight_sum(keep, exchange(send, 1, "sec"))
    rows, grad_w_kv = lax.optimization_barrier((rows, grad_w_kv))
    grad_inputs = lay_rows(place, rows)
    return dq[None], grad_inputs, grad_w_kv


def solution(mesh):
    in_specs = (
        P("sec", None, "lane"),
        P("sec", None, "lane"),
        P("sec", None, "lane"),
        P("sec", None),
        P("sec", None, None),
    )
    out_specs = (P("sec", None, "lane"), P(("sec", "lane"), None), P("sec", None, "lane"))
    return jax.shard_map(local, mesh=mesh, in_specs=in_specs, out_specs=out_specs, check_vma=False)
```

```python
import functools

import jax
import jax.numpy as jnp
from jax import lax
from jax.experimental import pallas as pl
from jax.experimental.pallas import tpu as pltpu
from jax.sharding import PartitionSpec as P

NQH = 40
KVH = 8
HD = 128
LOG2E = 1.4426950408889634
F32 = jnp.float32
BF16 = jnp.bfloat16
NN = (((1,), (0,)), ((), ()))
NT = (((1,), (1,)), ((), ()))
TN = (((0,), (0,)), ((), ()))
VMEM_BYTES = 24 * 1024 * 1024
ATTEND_VMEM_BYTES = 16 * 1024
SEG = 128
UNIT = 2


def dot(a, b, dims):
    return lax.dot_general(a, b, dims, preferred_element_type=F32)


def params(limit=VMEM_BYTES):
    return pltpu.CompilerParams(vmem_limit_bytes=limit)


def exchange(x, offset, axis):
    return lax.ppermute(x, axis, [(i, i ^ offset) for i in range(lax.axis_size(axis))])


def key_blocks(keys, qlen):
    first = keys - qlen
    blocks = []
    at = 0
    while at < keys:
        size = 2 * SEG if at + 2 * SEG <= first + SEG else SEG
        blocks.append((at, size, sum(first + qlen - t * SEG > at for t in range(qlen // SEG))))
        at += size
    return blocks


def attend_kernel(n, group, aliased, place, *refs):
    kv, refs = refs[:n], refs[n:]
    q_ref, do_ref = refs[:2]
    dq_ref, keep_ref, send_ref = refs[2 + aliased : 5 + aliased]
    k_s, v_s, q_s, do_s, qt_s, dot_s, s_s, dp_s, top_s, sum_s, weighted_s, acc = refs[5 + aliased :]
    qlen = q_ref.shape[0]
    keys = k_s.shape[0]
    blk = keys // n
    first = keys - qlen
    segments = qlen // SEG
    scale = HD**-0.5
    factor = scale * LOG2E
    me = place[0]

    def place_of(b):
        return pl.multiple_of(lax.bitwise_xor(me, b) * blk, blk)

    for b in range(n):
        k_s[pl.ds(place_of(b), blk), :] = kv[b][:, :HD]
        v_s[pl.ds(place_of(b), blk), :] = kv[b][:, HD:]

    units = [range(h, min(h + UNIT, group)) for h in range(0, group, UNIT)]
    at = 0
    for unit in units:
        for t in range(segments):
            low = qlen - (t + 1) * SEG
            for h in unit:
                x = q_ref[low : low + SEG, h * HD : (h + 1) * HD]
                y = do_ref[low : low + SEG, h * HD : (h + 1) * HD]
                q_s[at : at + SEG, :] = x
                do_s[at : at + SEG, :] = y
                qt_s[:, at : at + SEG] = x.T
                dot_s[:, at : at + SEG] = y.T
                at += SEG

    def spread(x):
        return jnp.broadcast_to(x, (x.shape[0], SEG))

    base = 0
    for index, unit in enumerate(units):
        width = len(unit) * SEG
        whole = width * segments
        blocks = [(k0, size, seen * width) for k0, size, seen in key_blocks(keys, qlen)]

        for k0, size, high in blocks:
            s = dot(q_s[base : base + high, :], k_s[k0 : k0 + size, :], NT)
            top = None
            for k in range(k0, k0 + size, SEG):
                piece = s[:, k - k0 : k - k0 + SEG]
                last = first + qlen - high // width * SEG
                if k + SEG - 1 > last:
                    edge = piece[high - width :]
                    key = k + lax.broadcasted_iota(jnp.int32, edge.shape, 1)
                    row = last + lax.rem(lax.broadcasted_iota(jnp.int32, edge.shape, 0), SEG)
                    edge = jnp.where(key <= row, edge, -jnp.inf)
                    piece = edge if high == width else jnp.concatenate([piece[: high - width], edge], axis=0)
                s_s[:high, k : k + SEG] = piece
                top = piece if top is None else jnp.maximum(top, piece)
            top_s[:high, :] = top if k0 == 0 else jnp.maximum(top_s[:high, :], top)
        top_s[:whole, :] = spread(jnp.max(top_s[:whole, :], axis=1, keepdims=True) * factor)

        for k0, size, high in blocks:
            dp = dot(do_s[base : base + high, :], v_s[k0 : k0 + size, :], NT)
            total = weighted = None
            for k in range(k0, k0 + size, SEG):
                p = jnp.exp2(s_s[:high, k : k + SEG] * factor - top_s[:high, :])
                s_s[:high, k : k + SEG] = p
                piece = dp[:, k - k0 : k - k0 + SEG]
                dp_s[:high, k : k + SEG] = piece
                total = p if total is None else total + p
                weighted = p * piece if weighted is None else weighted + p * piece
            sum_s[:high, :] = total if k0 == 0 else sum_s[:high, :] + total
            weighted_s[:high, :] = weighted if k0 == 0 else weighted_s[:high, :] + weighted
        inverse = 1.0 / jnp.sum(sum_s[:whole, :], axis=1, keepdims=True)
        delta = jnp.sum(weighted_s[:whole, :], axis=1, keepdims=True) * inverse
        sum_s[:whole, :] = spread(inverse)
        weighted_s[:whole, :] = spread(delta)

        dq = None
        for k0, size, high in blocks:
            low_parts, ds_parts = [], []
            for k in range(k0, k0 + size, SEG):
                p = s_s[:high, k : k + SEG] * sum_s[:high, :]
                ds_parts.append((p * (dp_s[:high, k : k + SEG] - weighted_s[:high, :])).astype(BF16))
                low_parts.append(p.astype(BF16))
            low = jnp.concatenate(low_parts, axis=1)
            ds = jnp.concatenate(ds_parts, axis=1)
            dv = dot(dot_s[:, base : base + high], low, NN)
            dk = dot(qt_s[:, base : base + high], ds, NN)
            if index:
                dv = acc[HD:, k0 : k0 + size] + dv
                dk = acc[:HD, k0 : k0 + size] + dk
            acc[HD:, k0 : k0 + size] = dv
            acc[:HD, k0 : k0 + size] = dk
            part = dot(ds, k_s[k0 : k0 + size, :], NN)
            if dq is None:
                dq = part
            elif high == whole:
                dq = dq + part
            else:
                dq = jnp.concatenate([dq[:high] + part, dq[high:]], axis=0)
        dq = (dq * scale).astype(BF16)
        at = 0
        for t in range(segments):
            low = qlen - (t + 1) * SEG
            for h in unit:
                dq_ref[low : low + SEG, h * HD : (h + 1) * HD] = dq[at : at + SEG]
                at += SEG
        base += whole

    for b in range(n):
        dk = acc[:HD, pl.ds(place_of(b), blk)] * scale
        dv = acc[HD:, pl.ds(place_of(b), blk)]
        if b % 2:
            send_ref[b // 2, :HD, :] = dk.astype(BF16)
            send_ref[b // 2, HD:, :] = dv.astype(BF16)
        else:
            keep_ref[b // 2, :HD, :] = dk
            keep_ref[b // 2, HD:, :] = dv


def attend(place, kv, head, q, do, dq, group):
    n = len(kv)
    blk, width = kv[0].shape[0], 2 * HD
    qlen = q.shape[0]
    keys = n * blk
    column = pl.BlockSpec((qlen, group * HD), lambda i, s: (0, head))
    full = lambda shape: pl.BlockSpec(shape, lambda i, s: (0,) * len(shape))
    in_specs = [pl.BlockSpec((blk, width), lambda i, s: (0, head))] * n + [column, column]
    operands = [*kv, q, do]
    aliases = {}
    if dq is not None:
        aliases = {1 + len(operands): 0}
        operands.append(dq)
        in_specs.append(pl.BlockSpec(memory_space=pl.ANY))
    rows = min(UNIT, group) * qlen
    parts = (n // 2, width, blk)
    work = group * qlen * keys * HD * 10
    return pl.pallas_call(
        functools.partial(attend_kernel, n, group, dq is not None),
        grid_spec=pltpu.PrefetchScalarGridSpec(
            num_scalar_prefetch=1,
            grid=(1,),
            in_specs=in_specs,
            out_specs=[column, full(parts), full(parts)],
            scratch_shapes=[
                pltpu.VMEM((keys, HD), BF16),
                pltpu.VMEM((keys, HD), BF16),
                pltpu.VMEM((group * qlen, HD), BF16),
                pltpu.VMEM((group * qlen, HD), BF16),
                pltpu.VMEM((HD, group * qlen), BF16),
                pltpu.VMEM((HD, group * qlen), BF16),
                pltpu.VMEM((rows, keys), F32),
                pltpu.VMEM((rows, keys), F32),
                pltpu.VMEM((rows, SEG), F32),
                pltpu.VMEM((rows, SEG), F32),
                pltpu.VMEM((rows, SEG), F32),
                pltpu.VMEM((width, keys), F32),
            ],
        ),
        out_shape=[
            jax.ShapeDtypeStruct(q.shape, BF16),
            jax.ShapeDtypeStruct(parts, F32),
            jax.ShapeDtypeStruct(parts, BF16),
        ],
        input_output_aliases=aliases,
        compiler_params=params(keys * ATTEND_VMEM_BYTES),
        cost_estimate=pl.CostEstimate(flops=work * 2, bytes_accessed=8 * keys * width, transcendentals=0),
        name="attend",
    )(place, *operands)


def pair_sum_kernel(keep_ref, got_ref, own_ref, *send_refs):
    own_ref[...] = keep_ref[0] + got_ref[0].astype(F32)
    for k, send_ref in enumerate(send_refs, 1):
        send_ref[...] = (keep_ref[k] + got_ref[k].astype(F32)).astype(BF16)


def pair_sum(keep, got):
    half, width, blk = keep.shape
    out_shape = [jax.ShapeDtypeStruct((width, blk), F32)]
    out_shape += [jax.ShapeDtypeStruct((width, blk), BF16)] * (half - 1)
    return pl.pallas_call(
        pair_sum_kernel, out_shape=out_shape, compiler_params=params(), name="pair_sum"
    )(keep, got)


def owner_sum_kernel(heads, lanes, place, *refs):
    part_refs, sum_ref, lane_refs = refs[: -1 - lanes], refs[-1 - lanes], refs[-lanes:]
    each = len(part_refs) // heads
    for a in range(heads):
        own_ref, *got_refs = part_refs[a * each : (a + 1) * each]
        total = own_ref[...]
        for got_ref in got_refs:
            total = total + got_ref[...].astype(F32)
        sum_ref[:, a * 2 * HD : (a + 1) * 2 * HD] = total.astype(BF16).T
    rows = lane_refs[0].shape[0]
    for b, lane_ref in enumerate(lane_refs):
        start = pl.multiple_of(lax.bitwise_xor(place[1], b) * rows, rows)
        lane_ref[...] = sum_ref[pl.ds(start, rows), :]


def owner_sum(place, parts, lanes):
    heads = len(parts)
    width, blk = parts[0][0].shape
    parts = [x for head in parts for x in head]
    out_shape = [jax.ShapeDtypeStruct((blk, heads * width), BF16)]
    out_shape += [jax.ShapeDtypeStruct((blk // lanes, heads * width), BF16)] * lanes
    return pl.pallas_call(
        functools.partial(owner_sum_kernel, heads, lanes),
        in_specs=[pl.BlockSpec(memory_space=pltpu.SMEM)]
        + [pl.BlockSpec(memory_space=pltpu.VMEM)] * len(parts),
        out_shape=out_shape,
        compiler_params=params(),
        name="owner_sum",
    )(place, *parts)


def weight_grad_kernel(half, place, *refs):
    x_refs, grad_refs, keep_ref, send_ref = refs[:half], refs[half:-2], refs[-2], refs[-1]
    cols = keep_ref.shape[0]
    mine = lax.rem(place[0], 2)
    for order, out_ref in enumerate((keep_ref, send_ref)):
        start = pl.multiple_of(lax.bitwise_xor(mine, order) * cols, HD)
        total = None
        for x_ref, grad_ref in zip(x_refs, grad_refs):
            part = dot(x_ref[:, pl.ds(start, cols)], grad_ref[...], TN)
            total = part if total is None else total + part
        out_ref[...] = total


def weight_grad(place, columns, gathered):
    half = len(columns)
    cols = columns[0].shape[1] // 2
    shape = jax.ShapeDtypeStruct((cols, gathered[0].shape[1]), F32)
    return pl.pallas_call(
        functools.partial(weight_grad_kernel, half),
        in_specs=[pl.BlockSpec(memory_space=pltpu.SMEM)] + [pl.BlockSpec(memory_space=pltpu.VMEM)] * (2 * half),
        out_shape=[shape, shape],
        compiler_params=params(),
        name="weight_grad",
    )(place, *columns, *gathered)


def weight_sum_kernel(heads, keep_ref, got_ref, out_ref):
    for a in range(heads):
        for c in range(2):
            span = pl.ds((2 * a + c) * HD, HD)
            out_ref[:, c, a * HD : (a + 1) * HD] = keep_ref[:, span] + got_ref[:, span]


def weight_sum(keep, got):
    cols, features = keep.shape
    heads = features // (2 * HD)
    return pl.pallas_call(
        functools.partial(weight_sum_kernel, heads),
        out_shape=jax.ShapeDtypeStruct((cols, 2, heads * HD), F32),
        compiler_params=params(),
        name="weight_sum",
    )(keep, got)


def input_grad_kernel(heads, half, lanes, place, *refs):
    block_refs, refs = refs[:half], refs[half:]
    w_refs, out_refs, left = refs[:2], refs[2 : 2 + half], refs[2 + half]
    me, lane = place[0], place[1]
    rows = block_refs[0].shape[1]
    width = w_refs[0].shape[0]
    features = w_refs[0].shape[1] // 2
    for k in range(half):
        for b in range(lanes):
            for a in range(heads):
                head = lax.bitwise_xor(lane, b) * heads + a
                for c in range(2):
                    start = pl.multiple_of(c * features + head * HD, HD)
                    span = pl.ds((2 * a + c) * HD, HD)
                    left[k * rows : (k + 1) * rows, pl.ds(start, HD)] = block_refs[k][b, :, span]
    mine = lax.rem(me, 2)
    for order, w_ref in enumerate(w_refs):
        start = pl.multiple_of(lax.bitwise_xor(mine, order) * width, HD)
        result = dot(left[...], w_ref[...], NT).astype(BF16)
        for k in range(half):
            out_refs[k][:, pl.ds(start, width)] = result[k * rows : (k + 1) * rows]


def input_grad(place, blocks, own_w, other_w):
    half = len(blocks)
    lanes, rows, here = blocks[0].shape
    width, features = own_w.shape
    return pl.pallas_call(
        functools.partial(input_grad_kernel, here // (2 * HD), half, lanes),
        in_specs=[pl.BlockSpec(memory_space=pltpu.SMEM)]
        + [pl.BlockSpec(memory_space=pltpu.VMEM)] * (len(blocks) + 2),
        out_shape=[jax.ShapeDtypeStruct((rows, 2 * width), BF16)] * half,
        scratch_shapes=[pltpu.VMEM((half * rows, features), BF16)],
        compiler_params=params(),
        name="input_grad",
    )(place, *blocks, own_w, other_w)


def lay_rows_kernel(place, *refs):
    blocks, out_ref, sems = refs[:-2], refs[-2], refs[-1]
    width = blocks[0].shape[1]
    chip = lax.div(place[0], 2)
    copies = []
    for k, block in enumerate(blocks):
        start = pl.multiple_of(lax.bitwise_xor(chip, k) * width, HD)
        copies.append(pltpu.make_async_copy(block, out_ref.at[:, pl.ds(start, width)], sems.at[k]))
        copies[-1].start()
    for copy in copies:
        copy.wait()


def lay_rows(place, blocks):
    rows, width = blocks[0].shape
    count = len(blocks)
    return pl.pallas_call(
        lay_rows_kernel,
        in_specs=[pl.BlockSpec(memory_space=pltpu.SMEM)] + [pl.BlockSpec(memory_space=pl.ANY)] * count,
        out_specs=pl.BlockSpec(memory_space=pl.ANY),
        out_shape=jax.ShapeDtypeStruct((rows, width * count), BF16),
        scratch_shapes=[pltpu.SemaphoreType.DMA((count,))],
        compiler_params=params(),
        name="lay_rows",
    )(place, *blocks)


def local(queries, key_value, grad_out, inputs, w_kv):
    n = lax.axis_size("sec")
    lanes = lax.axis_size("lane")
    me = lax.axis_index("sec")
    place = jnp.stack([me, lax.axis_index("lane")]).astype(jnp.int32)
    heads = key_value.shape[2] // HD
    group = NQH // KVH
    half = n // 2
    q, do = queries[0], grad_out[0]

    def across(blocks):
        return [blocks[0]] + [exchange(blocks[k], 2 * k, "sec") for k in range(1, half)]

    own = jnp.concatenate(
        [key_value[:, c, a * HD : (a + 1) * HD] for a in range(heads) for c in range(2)], axis=1
    )
    near = across([own] * half)
    kv = [x for block in near for x in (block, exchange(block, 1, "sec"))]

    cols = 2 * inputs.shape[1] // n
    columns = [
        lax.dynamic_slice_in_dim(inputs, lax.bitwise_xor(me // 2, k) * cols, cols, axis=1)
        for k in range(half)
    ]
    columns, near = lax.optimization_barrier((columns, near))
    columns = across(columns)
    own_w = w_kv.reshape(w_kv.shape[0], -1)
    other_w = exchange(own_w, 1, "sec")

    dq = None
    keeps, gots = [], []
    for a in range(heads):
        dq, keep, send = attend(place, kv, a, q, do, dq, group)
        if a == heads - 1:
            keep, columns[1:] = lax.optimization_barrier((keep, columns[1:]))
        keeps.append(keep)
        gots.append(exchange(send, 1, "sec"))

    parts = [across(pair_sum(keep, got)) for keep, got in zip(keeps, gots)]
    mine, *by_lane = owner_sum(place, parts, lanes)
    by_lane[1:] = [exchange(by_lane[b], b, "lane") for b in range(1, lanes)]
    gathered = across([mine] * half)
    blocks = across([jnp.stack(by_lane)] * half)
    blocks, gathered = lax.optimization_barrier((blocks, gathered))

    rows = list(input_grad(place, blocks, own_w, other_w))
    rows[0], gathered = lax.optimization_barrier((rows[0], gathered))
    rows = across(rows)
    keep, send = weight_grad(place, columns, gathered)
    grad_w_kv = weight_sum(keep, exchange(send, 1, "sec"))
    rows, grad_w_kv = lax.optimization_barrier((rows, grad_w_kv))
    grad_inputs = lay_rows(place, rows)
    return dq[None], grad_inputs, grad_w_kv


def solution(mesh):
    in_specs = (
        P("sec", None, "lane"),
        P("sec", None, "lane"),
        P("sec", None, "lane"),
        P("sec", None),
        P("sec", None, None),
    )
    out_specs = (P("sec", None, "lane"), P(("sec", "lane"), None), P("sec", None, "lane"))
    return jax.shard_map(local, mesh=mesh, in_specs=in_specs, out_specs=out_specs, check_vma=False)
```

```python
import functools

import jax
import jax.numpy as jnp
from jax import lax
from jax.experimental import pallas as pl
from jax.experimental.pallas import tpu as pltpu
from jax.sharding import PartitionSpec as P

NQH = 40
KVH = 8
HD = 128
LOG2E = 1.4426950408889634
F32 = jnp.float32
BF16 = jnp.bfloat16
NN = (((1,), (0,)), ((), ()))
NT = (((1,), (1,)), ((), ()))
TN = (((0,), (0,)), ((), ()))
VMEM_BYTES = 24 * 1024 * 1024
ATTEND_VMEM_BYTES = 16 * 1024
SEG = 128
UNIT = 2


def dot(a, b, dims):
    return lax.dot_general(a, b, dims, preferred_element_type=F32)


def params(limit=VMEM_BYTES):
    return pltpu.CompilerParams(vmem_limit_bytes=limit)


def exchange(x, offset, axis):
    return lax.ppermute(x, axis, [(i, i ^ offset) for i in range(lax.axis_size(axis))])


def key_blocks(keys, qlen):
    first = keys - qlen
    blocks = []
    at = 0
    while at < keys:
        size = 2 * SEG if at + 2 * SEG <= first + SEG else SEG
        blocks.append((at, size, sum(first + qlen - t * SEG > at for t in range(qlen // SEG))))
        at += size
    return blocks


def attend_kernel(n, group, aliased, place, *refs):
    kv, refs = refs[:n], refs[n:]
    q_ref, do_ref = refs[:2]
    dq_ref, keep_ref, send_ref = refs[2 + aliased : 5 + aliased]
    k_s, v_s, q_s, do_s, qt_s, dot_s, s_s, dp_s, top_s, sum_s, weighted_s, acc = refs[5 + aliased :]
    qlen = q_ref.shape[0]
    keys = k_s.shape[0]
    blk = keys // n
    first = keys - qlen
    segments = qlen // SEG
    scale = HD**-0.5
    factor = scale * LOG2E
    me = place[0]

    def place_of(b):
        return pl.multiple_of(lax.bitwise_xor(me, b) * blk, blk)

    for b in range(n):
        k_s[pl.ds(place_of(b), blk), :] = kv[b][:, :HD]
        v_s[pl.ds(place_of(b), blk), :] = kv[b][:, HD:]

    units = [range(h, min(h + UNIT, group)) for h in range(0, group, UNIT)]
    at = 0
    for unit in units:
        for t in range(segments):
            low = qlen - (t + 1) * SEG
            for h in unit:
                x = q_ref[low : low + SEG, h * HD : (h + 1) * HD]
                y = do_ref[low : low + SEG, h * HD : (h + 1) * HD]
                q_s[at : at + SEG, :] = x
                do_s[at : at + SEG, :] = y
                qt_s[:, at : at + SEG] = x.T
                dot_s[:, at : at + SEG] = y.T
                at += SEG

    def spread(x):
        return jnp.broadcast_to(x, (x.shape[0], SEG))

    base = 0
    for index, unit in enumerate(units):
        width = len(unit) * SEG
        whole = width * segments
        blocks = [(k0, size, seen * width) for k0, size, seen in key_blocks(keys, qlen)]

        for k0, size, high in blocks:
            s = dot(q_s[base : base + high, :], k_s[k0 : k0 + size, :], NT)
            top = None
            for k in range(k0, k0 + size, SEG):
                piece = s[:, k - k0 : k - k0 + SEG]
                last = first + qlen - high // width * SEG
                if k + SEG - 1 > last:
                    edge = piece[high - width :]
                    key = k + lax.broadcasted_iota(jnp.int32, edge.shape, 1)
                    row = last + lax.rem(lax.broadcasted_iota(jnp.int32, edge.shape, 0), SEG)
                    edge = jnp.where(key <= row, edge, -jnp.inf)
                    piece = edge if high == width else jnp.concatenate([piece[: high - width], edge], axis=0)
                s_s[:high, k : k + SEG] = piece
                top = piece if top is None else jnp.maximum(top, piece)
            top_s[:high, :] = top if k0 == 0 else jnp.maximum(top_s[:high, :], top)
        top_s[:whole, :] = spread(jnp.max(top_s[:whole, :], axis=1, keepdims=True) * factor)

        for k0, size, high in blocks:
            dp = dot(do_s[base : base + high, :], v_s[k0 : k0 + size, :], NT)
            total = weighted = None
            for k in range(k0, k0 + size, SEG):
                p = jnp.exp2(s_s[:high, k : k + SEG] * factor - top_s[:high, :])
                s_s[:high, k : k + SEG] = p
                piece = dp[:, k - k0 : k - k0 + SEG]
                dp_s[:high, k : k + SEG] = piece
                total = p if total is None else total + p
                weighted = p * piece if weighted is None else weighted + p * piece
            sum_s[:high, :] = total if k0 == 0 else sum_s[:high, :] + total
            weighted_s[:high, :] = weighted if k0 == 0 else weighted_s[:high, :] + weighted
        inverse = 1.0 / jnp.sum(sum_s[:whole, :], axis=1, keepdims=True)
        delta = jnp.sum(weighted_s[:whole, :], axis=1, keepdims=True) * inverse
        sum_s[:whole, :] = spread(inverse)
        weighted_s[:whole, :] = spread(delta)

        dq = None
        for k0, size, high in blocks:
            low_parts, ds_parts = [], []
            for k in range(k0, k0 + size, SEG):
                p = s_s[:high, k : k + SEG] * sum_s[:high, :]
                ds_parts.append((p * (dp_s[:high, k : k + SEG] - weighted_s[:high, :])).astype(BF16))
                low_parts.append(p.astype(BF16))
            low = jnp.concatenate(low_parts, axis=1)
            ds = jnp.concatenate(ds_parts, axis=1)
            dv = dot(dot_s[:, base : base + high], low, NN)
            dk = dot(qt_s[:, base : base + high], ds, NN)
            if index:
                dv = acc[HD:, k0 : k0 + size] + dv
                dk = acc[:HD, k0 : k0 + size] + dk
            acc[HD:, k0 : k0 + size] = dv
            acc[:HD, k0 : k0 + size] = dk
            part = dot(ds, k_s[k0 : k0 + size, :], NN)
            if dq is None:
                dq = part
            elif high == whole:
                dq = dq + part
            else:
                dq = jnp.concatenate([dq[:high] + part, dq[high:]], axis=0)
        dq = (dq * scale).astype(BF16)
        at = 0
        for t in range(segments):
            low = qlen - (t + 1) * SEG
            for h in unit:
                dq_ref[low : low + SEG, h * HD : (h + 1) * HD] = dq[at : at + SEG]
                at += SEG
        base += whole

    for b in range(n):
        dk = acc[:HD, pl.ds(place_of(b), blk)] * scale
        dv = acc[HD:, pl.ds(place_of(b), blk)]
        if b % 2:
            send_ref[b // 2, :HD, :] = dk.astype(BF16)
            send_ref[b // 2, HD:, :] = dv.astype(BF16)
        else:
            keep_ref[b // 2, :HD, :] = dk
            keep_ref[b // 2, HD:, :] = dv


def attend(place, kv, head, q, do, dq, group):
    n = len(kv)
    blk, width = kv[0].shape[0], 2 * HD
    qlen = q.shape[0]
    keys = n * blk
    column = pl.BlockSpec((qlen, group * HD), lambda i, s: (0, head))
    full = lambda shape: pl.BlockSpec(shape, lambda i, s: (0,) * len(shape))
    in_specs = [pl.BlockSpec((blk, width), lambda i, s: (0, head))] * n + [column, column]
    operands = [*kv, q, do]
    aliases = {}
    if dq is not None:
        aliases = {1 + len(operands): 0}
        operands.append(dq)
        in_specs.append(pl.BlockSpec(memory_space=pl.ANY))
    rows = min(UNIT, group) * qlen
    parts = (n // 2, width, blk)
    work = group * qlen * keys * HD * 10
    return pl.pallas_call(
        functools.partial(attend_kernel, n, group, dq is not None),
        grid_spec=pltpu.PrefetchScalarGridSpec(
            num_scalar_prefetch=1,
            grid=(1,),
            in_specs=in_specs,
            out_specs=[column, full(parts), full(parts)],
            scratch_shapes=[
                pltpu.VMEM((keys, HD), BF16),
                pltpu.VMEM((keys, HD), BF16),
                pltpu.VMEM((group * qlen, HD), BF16),
                pltpu.VMEM((group * qlen, HD), BF16),
                pltpu.VMEM((HD, group * qlen), BF16),
                pltpu.VMEM((HD, group * qlen), BF16),
                pltpu.VMEM((rows, keys), F32),
                pltpu.VMEM((rows, keys), F32),
                pltpu.VMEM((rows, SEG), F32),
                pltpu.VMEM((rows, SEG), F32),
                pltpu.VMEM((rows, SEG), F32),
                pltpu.VMEM((width, keys), F32),
            ],
        ),
        out_shape=[
            jax.ShapeDtypeStruct(q.shape, BF16),
            jax.ShapeDtypeStruct(parts, F32),
            jax.ShapeDtypeStruct(parts, BF16),
        ],
        input_output_aliases=aliases,
        compiler_params=params(keys * ATTEND_VMEM_BYTES),
        cost_estimate=pl.CostEstimate(flops=work * 2, bytes_accessed=8 * keys * width, transcendentals=0),
        name="attend",
    )(place, *operands)


def pair_sum_kernel(keep_ref, got_ref, own_ref, *send_refs):
    own_ref[...] = keep_ref[0] + got_ref[0].astype(F32)
    for k, send_ref in enumerate(send_refs, 1):
        send_ref[...] = (keep_ref[k] + got_ref[k].astype(F32)).astype(BF16)


def pair_sum(keep, got):
    half, width, blk = keep.shape
    out_shape = [jax.ShapeDtypeStruct((width, blk), F32)]
    out_shape += [jax.ShapeDtypeStruct((width, blk), BF16)] * (half - 1)
    return pl.pallas_call(
        pair_sum_kernel, out_shape=out_shape, compiler_params=params(), name="pair_sum"
    )(keep, got)


def owner_sum_kernel(heads, lanes, place, *refs):
    part_refs, sum_ref, lane_refs = refs[: -1 - lanes], refs[-1 - lanes], refs[-lanes:]
    each = len(part_refs) // heads
    for a in range(heads):
        own_ref, *got_refs = part_refs[a * each : (a + 1) * each]
        total = own_ref[...]
        for got_ref in got_refs:
            total = total + got_ref[...].astype(F32)
        sum_ref[:, a * 2 * HD : (a + 1) * 2 * HD] = total.astype(BF16).T
    rows = lane_refs[0].shape[0]
    for b, lane_ref in enumerate(lane_refs):
        start = pl.multiple_of(lax.bitwise_xor(place[1], b) * rows, rows)
        lane_ref[...] = sum_ref[pl.ds(start, rows), :]


def owner_sum(place, parts, lanes):
    heads = len(parts)
    width, blk = parts[0][0].shape
    parts = [x for head in parts for x in head]
    out_shape = [jax.ShapeDtypeStruct((blk, heads * width), BF16)]
    out_shape += [jax.ShapeDtypeStruct((blk // lanes, heads * width), BF16)] * lanes
    return pl.pallas_call(
        functools.partial(owner_sum_kernel, heads, lanes),
        in_specs=[pl.BlockSpec(memory_space=pltpu.SMEM)]
        + [pl.BlockSpec(memory_space=pltpu.VMEM)] * len(parts),
        out_shape=out_shape,
        compiler_params=params(),
        name="owner_sum",
    )(place, *parts)


def weight_grad_kernel(half, place, *refs):
    x_refs, grad_refs, keep_ref, send_ref = refs[:half], refs[half:-2], refs[-2], refs[-1]
    cols = keep_ref.shape[0]
    mine = lax.rem(place[0], 2)
    for order, out_ref in enumerate((keep_ref, send_ref)):
        start = pl.multiple_of(lax.bitwise_xor(mine, order) * cols, HD)
        total = None
        for x_ref, grad_ref in zip(x_refs, grad_refs):
            part = dot(x_ref[:, pl.ds(start, cols)], grad_ref[...], TN)
            total = part if total is None else total + part
        out_ref[...] = total


def weight_grad(place, columns, gathered):
    half = len(columns)
    rows, cols = columns[1].shape
    features = gathered[0].shape[1]
    shape = jax.ShapeDtypeStruct((cols // 2, features), F32)
    full = lambda *shape: pl.BlockSpec(shape, lambda i, s: (0, 0))
    return pl.pallas_call(
        functools.partial(weight_grad_kernel, half),
        grid_spec=pltpu.PrefetchScalarGridSpec(
            num_scalar_prefetch=1,
            grid=(1,),
            in_specs=[pl.BlockSpec((rows, cols), lambda i, s: (0, lax.div(s[0], 2)))]
            + [full(rows, cols)] * (half - 1)
            + [full(rows, features)] * half,
            out_specs=[full(*shape.shape)] * 2,
        ),
        out_shape=[shape, shape],
        compiler_params=params(),
        name="weight_grad",
    )(place, *columns, *gathered)


def weight_sum_kernel(heads, keep_ref, got_ref, out_ref):
    for a in range(heads):
        for c in range(2):
            span = pl.ds((2 * a + c) * HD, HD)
            out_ref[:, c, a * HD : (a + 1) * HD] = keep_ref[:, span] + got_ref[:, span]


def weight_sum(keep, got):
    cols, features = keep.shape
    heads = features // (2 * HD)
    return pl.pallas_call(
        functools.partial(weight_sum_kernel, heads),
        out_shape=jax.ShapeDtypeStruct((cols, 2, heads * HD), F32),
        compiler_params=params(),
        name="weight_sum",
    )(keep, got)


def input_grad_kernel(heads, half, lanes, place, *refs):
    block_refs, refs = refs[:half], refs[half:]
    w_refs, out_refs, left = refs[:2], refs[2 : 2 + half], refs[2 + half]
    me, lane = place[0], place[1]
    rows = block_refs[0].shape[1]
    width = w_refs[0].shape[0]
    features = w_refs[0].shape[1] // 2
    for k in range(half):
        for b in range(lanes):
            for a in range(heads):
                head = lax.bitwise_xor(lane, b) * heads + a
                for c in range(2):
                    start = pl.multiple_of(c * features + head * HD, HD)
                    span = pl.ds((2 * a + c) * HD, HD)
                    left[k * rows : (k + 1) * rows, pl.ds(start, HD)] = block_refs[k][b, :, span]
    mine = lax.rem(me, 2)
    for order, w_ref in enumerate(w_refs):
        start = pl.multiple_of(lax.bitwise_xor(mine, order) * width, HD)
        result = dot(left[...], w_ref[...], NT).astype(BF16)
        for k in range(half):
            out_refs[k][:, pl.ds(start, width)] = result[k * rows : (k + 1) * rows]


def input_grad(place, blocks, own_w, other_w):
    half = len(blocks)
    lanes, rows, here = blocks[0].shape
    width, features = own_w.shape
    return pl.pallas_call(
        functools.partial(input_grad_kernel, here // (2 * HD), half, lanes),
        in_specs=[pl.BlockSpec(memory_space=pltpu.SMEM)]
        + [pl.BlockSpec(memory_space=pltpu.VMEM)] * (len(blocks) + 2),
        out_shape=[jax.ShapeDtypeStruct((rows, 2 * width), BF16)] * half,
        scratch_shapes=[pltpu.VMEM((half * rows, features), BF16)],
        compiler_params=params(),
        name="input_grad",
    )(place, *blocks, own_w, other_w)


def lay_rows_kernel(place, *refs):
    blocks, out_ref, sems = refs[:-2], refs[-2], refs[-1]
    width = blocks[0].shape[1]
    chip = lax.div(place[0], 2)
    copies = []
    for k, block in enumerate(blocks):
        start = pl.multiple_of(lax.bitwise_xor(chip, k) * width, HD)
        copies.append(pltpu.make_async_copy(block, out_ref.at[:, pl.ds(start, width)], sems.at[k]))
        copies[-1].start()
    for copy in copies:
        copy.wait()


def lay_rows(place, blocks):
    rows, width = blocks[0].shape
    count = len(blocks)
    return pl.pallas_call(
        lay_rows_kernel,
        in_specs=[pl.BlockSpec(memory_space=pltpu.SMEM)] + [pl.BlockSpec(memory_space=pl.ANY)] * count,
        out_specs=pl.BlockSpec(memory_space=pl.ANY),
        out_shape=jax.ShapeDtypeStruct((rows, width * count), BF16),
        scratch_shapes=[pltpu.SemaphoreType.DMA((count,))],
        compiler_params=params(),
        name="lay_rows",
    )(place, *blocks)


def local(queries, key_value, grad_out, inputs, w_kv):
    n = lax.axis_size("sec")
    lanes = lax.axis_size("lane")
    me = lax.axis_index("sec")
    place = jnp.stack([me, lax.axis_index("lane")]).astype(jnp.int32)
    heads = key_value.shape[2] // HD
    group = NQH // KVH
    half = n // 2
    q, do = queries[0], grad_out[0]

    def across(blocks):
        return [blocks[0]] + [exchange(blocks[k], 2 * k, "sec") for k in range(1, half)]

    own = jnp.concatenate(
        [key_value[:, c, a * HD : (a + 1) * HD] for a in range(heads) for c in range(2)], axis=1
    )
    near = across([own] * half)
    kv = [x for block in near for x in (block, exchange(block, 1, "sec"))]

    cols = 2 * inputs.shape[1] // n
    columns = [
        lax.dynamic_slice_in_dim(inputs, lax.bitwise_xor(me // 2, k) * cols, cols, axis=1)
        for k in range(1, half)
    ]
    columns, near = lax.optimization_barrier((columns, near))
    columns = across([inputs, *columns])
    own_w = w_kv.reshape(w_kv.shape[0], -1)
    other_w = exchange(own_w, 1, "sec")

    dq = None
    keeps, gots = [], []
    for a in range(heads):
        dq, keep, send = attend(place, kv, a, q, do, dq, group)
        if a == heads - 1:
            keep, columns[1:] = lax.optimization_barrier((keep, columns[1:]))
        keeps.append(keep)
        gots.append(exchange(send, 1, "sec"))

    parts = [across(pair_sum(keep, got)) for keep, got in zip(keeps, gots)]
    mine, *by_lane = owner_sum(place, parts, lanes)
    by_lane[1:] = [exchange(by_lane[b], b, "lane") for b in range(1, lanes)]
    gathered = across([mine] * half)
    blocks = across([jnp.stack(by_lane)] * half)
    blocks, gathered = lax.optimization_barrier((blocks, gathered))

    rows = list(input_grad(place, blocks, own_w, other_w))
    rows[0], gathered = lax.optimization_barrier((rows[0], gathered))
    rows = across(rows)
    keep, send = weight_grad(place, columns, gathered)
    grad_w_kv = weight_sum(keep, exchange(send, 1, "sec"))
    rows, grad_w_kv = lax.optimization_barrier((rows, grad_w_kv))
    grad_inputs = lay_rows(place, rows)
    return dq[None], grad_inputs, grad_w_kv


def solution(mesh):
    in_specs = (
        P("sec", None, "lane"),
        P("sec", None, "lane"),
        P("sec", None, "lane"),
        P("sec", None),
        P("sec", None, None),
    )
    out_specs = (P("sec", None, "lane"), P(("sec", "lane"), None), P("sec", None, "lane"))
    return jax.shard_map(local, mesh=mesh, in_specs=in_specs, out_specs=out_specs, check_vma=False)
```
